32 devices in a mesh: rep: 16 (over z, y, x), tp: 2 (over core).
Axes of the slice: x: 2, y: 2, z: 4, core: 2. Of those that a mesh axis runs over, the one named last changes fastest.
Arguments:
- hidden: bfloat16 [512, 4, 5120], P('rep', None, 'tp'), may hold values from -6 to 6
- queries: bfloat16 [512, 4, 8192], P('rep', None, 'tp'), may hold values from -128 to 128
- key_cache: bfloat16 [512, 256, 1024], P('rep', None, 'tp'), may hold values from -4 to 4
- value_cache: bfloat16 [512, 256, 1024], P('rep', None, 'tp'), may hold values from -4 to 4
- lengths: int32 [512], P('rep'), may hold values from 2 to 256, as said below
- adopt: int32 [16], P('rep'), may hold values from 0 to 4
- old_kv: bfloat16 [5120, 2, 1024], P(None, None, 'tp'), may hold values from -0.078125 to 0.078125
- fresh_kv: bfloat16 [5120, 2, 1024], P('rep', None, 'tp'), may hold values from -0.078125 to 0.078125
Outputs:
- attended: bfloat16 [512, 4, 8192], P('rep', None, 'tp')
- appended: bfloat16 [512, 4, 2, 1024], P('rep', None, None, 'tp')
The draws below stay inside these ranges and needn't reach their ends.
Inputs may be any that keep to these rules, and one draw needn't show every extreme that they name: `lengths`: each replica's block of 32 rows has a row with 256 cached tokens.
All inputs are finite; a program needn't handle non-finite values.
Results may differ from the reference program's by a relative error of at most 0.0053.
Values may be sent and summed in bfloat16 or wider, within the bound.
A program may use at most 192 MiB of HBM per device.

```python
import jax
import jax.numpy as jnp
from jax import lax

D = 5120
QH = 64
KVH = 8
HEAD = 128
ROWS = 32
CTX = 256
STEPS = 4
REPLICAS = 16
ROWS_ALL = 512


def base_keys(key):
    return jnp.clip(jax.random.normal(key, (ROWS_ALL, CTX, KVH * HEAD), jnp.float32), -4.0, 4.0)


def draw_key_cache(key, part):
    shared = base_keys(key)
    return shared.astype(jnp.bfloat16)


def draw_queries(key, part):
    key = jax.random.fold_in(key, 5)
    shape = (ROWS_ALL, STEPS, QH * HEAD)
    drawn = jnp.clip(jax.random.normal(key, shape, jnp.float32), -6.0, 6.0)
    return drawn.astype(jnp.bfloat16)


def draw_lengths(key, part):
    key = jax.random.fold_in(key, 7)
    first_key, second_key = jax.random.split(key)
    drawn = jax.random.randint(first_key, (ROWS_ALL // ROWS, ROWS), 2, CTX + 1)
    fullest = jax.random.randint(second_key, (ROWS_ALL // ROWS, 1), 0, ROWS)
    positions = jnp.arange(ROWS, dtype=jnp.int32)[None, :]
    return jnp.where(positions == fullest, CTX, drawn).reshape(ROWS_ALL).astype(jnp.int32)


def plant(values, rng, smallest, top_value):
    longest = values.shape.index(max(values.shape))
    spots = []
    for shift in (0, 1):
        where = [jax.random.randint(jax.random.fold_in(rng, axis), (), 0, length) for axis, length in enumerate(values.shape)]
        where[longest] = (where[longest] + shift) % values.shape[longest]
        spots.append(tuple(where))
    return values.at[spots[0]].set(smallest).at[spots[1]].set(top_value)


def shard_levels(key, extent, cuts, least, largest):
    gain, own = 1.0, jax.random.fold_in(key, 6)
    for position, parts in cuts:
        draws = jnp.exp(jax.random.uniform(jax.random.fold_in(own, position), (parts,), jnp.float32, least / len(cuts), largest / len(cuts)))
        gain = gain * jnp.repeat(draws, extent[position] // parts).reshape([-1 if axis == position else 1 for axis in range(len(extent))])
    return gain


def scatter_about(stream_key, shape, spread, reach, cuts=(), kind=jnp.bfloat16):
    entries = spread * jax.random.normal(stream_key, shape, jnp.float32)
    if cuts:
        entries = entries * shard_levels(stream_key, shape, cuts, -0.22, 0.18)
    return jnp.clip(entries, -reach, reach).astype(kind)


def setup_inputs(seed: int = 0) -> dict:
    key_list = jax.random.split(jax.random.key(seed), 9)
    hidden = scatter_about(key_list[0], (ROWS_ALL, STEPS, D), 1.0, 6.0, ((0, 16), (2, 2)))
    queries = draw_queries(jax.random.fold_in(key_list[8], 71), 0)
    key_cache = draw_key_cache(jax.random.fold_in(key_list[8], 71), 0)
    value_cache = scatter_about(key_list[3], (ROWS_ALL, CTX, KVH * HEAD), 1.0, 4.0, ((0, 16), (2, 2)))
    lengths = draw_lengths(jax.random.fold_in(key_list[8], 71), 0)
    adopt = plant(jax.random.randint(key_list[5], (REPLICAS,), 0, STEPS + 1), jax.random.fold_in(key_list[5], 1), 0, STEPS).astype(jnp.int32)
    old_kv = scatter_about(key_list[6], (D, 2, KVH * HEAD), D ** -0.5, 0.078125, ((2, 2),))
    fresh_kv = scatter_about(key_list[7], (D, 2, KVH * HEAD), D ** -0.5, 0.078125, ((0, 16), (2, 2)))
    return {"hidden": hidden, "queries": queries, "key_cache": key_cache, "value_cache": value_cache, "lengths": lengths, "adopt": adopt, "old_kv": old_kv, "fresh_kv": fresh_kv}


epsilon = 1e-06

def attend(queries, key_cache, value_cache, lengths, fresh_keys, fresh_values):
    row_count = queries.shape[0]
    step_count = queries.shape[1]
    head_count = fresh_keys.shape[2]
    depth = fresh_keys.shape[3]
    context = key_cache.shape[1]
    grouped = queries.astype(jnp.float32).reshape(row_count, step_count, head_count, -1, depth)
    cached_keys = key_cache.astype(jnp.float32).reshape(row_count, context, head_count, depth)
    cached_values = value_cache.astype(jnp.float32).reshape(row_count, context, head_count, depth)
    new_keys = lax.optimization_barrier(fresh_keys).astype(jnp.float32)
    new_values = lax.optimization_barrier(fresh_values).astype(jnp.float32)
    scaling = depth ** (-0.5)
    cache_scores = jnp.einsum('rshgd,rthd->rshgt', grouped, cached_keys) * scaling
    fresh_scores = jnp.einsum('rshgd,rphd->rshgp', grouped, new_keys) * scaling
    visible_cache = (jnp.arange(context, dtype=jnp.int32)[None, :] < lengths[:, None])[:, None, None, None, :]
    stepping = jnp.arange(step_count, dtype=jnp.int32)
    visible_fresh = (stepping[None, :] <= stepping[:, None])[None, :, None, None, :]
    cache_scores = jnp.where(visible_cache, cache_scores, -1e+30)
    fresh_scores = jnp.where(visible_fresh, fresh_scores, -1e+30)
    highest = jnp.maximum(lax.optimization_barrier(jnp.max(cache_scores, axis=-1, keepdims=True)), lax.optimization_barrier(jnp.max(fresh_scores, axis=-1, keepdims=True)))
    cache_weights = jnp.where(visible_cache, jnp.exp(cache_scores - highest), 0.0)
    fresh_weights = jnp.where(visible_fresh, jnp.exp(fresh_scores - highest), 0.0)
    denominator = lax.optimization_barrier(jnp.sum(cache_weights, axis=-1, keepdims=True)) + lax.optimization_barrier(jnp.sum(fresh_weights, axis=-1, keepdims=True))
    cache_probs = lax.optimization_barrier((cache_weights / denominator).astype(jnp.bfloat16)).astype(jnp.float32)
    fresh_probs = lax.optimization_barrier((fresh_weights / denominator).astype(jnp.bfloat16)).astype(jnp.float32)
    mixed = jnp.einsum('rshgt,rthd->rshgd', cache_probs, cached_values)
    mixed = mixed + jnp.einsum('rshgp,rphd->rshgd', fresh_probs, new_values)
    return mixed.reshape(row_count, step_count, -1).astype(jnp.bfloat16)

def reference(hidden, queries, key_cache, value_cache, lengths, adopt, old_kv, fresh_kv):
    widened = hidden.astype(jnp.float32)
    normed = (widened * lax.rsqrt(lax.optimization_barrier(jnp.mean(widened * widened, axis=-1, keepdims=True)) + epsilon)).astype(jnp.bfloat16)
    flattened = normed.reshape(ROWS_ALL * STEPS, D)
    stale = jnp.dot(flattened, old_kv.reshape(D, 2 * KVH * HEAD), preferred_element_type=jnp.float32)
    current = jnp.dot(flattened, fresh_kv.reshape(D, 2 * KVH * HEAD), preferred_element_type=jnp.float32)
    stale = stale.reshape(ROWS_ALL, STEPS, 2 * KVH * HEAD)
    current = current.reshape(ROWS_ALL, STEPS, 2 * KVH * HEAD)
    owner = jnp.arange(ROWS_ALL, dtype=jnp.int32) // ROWS
    use_fresh = jnp.arange(STEPS, dtype=jnp.int32)[None, :] >= adopt[owner][:, None]
    chosen = jnp.where(use_fresh[:, :, None], current, stale).reshape(ROWS_ALL, STEPS, 2, KVH, HEAD)
    new_keys = chosen[:, :, 0]
    new_values = chosen[:, :, 1]
    new_keys = new_keys * lax.rsqrt(lax.optimization_barrier(jnp.mean(new_keys * new_keys, axis=-1, keepdims=True)) + epsilon)
    appended = jnp.stack([new_keys, new_values], axis=2).astype(jnp.bfloat16)

    def one_replica(bundle):
        return attend(bundle[0], bundle[1], bundle[2], bundle[3], bundle[4], bundle[5])
    bundle = (queries.reshape(REPLICAS, ROWS, STEPS, QH * HEAD), key_cache.reshape(REPLICAS, ROWS, CTX, KVH * HEAD), value_cache.reshape(REPLICAS, ROWS, CTX, KVH * HEAD), lengths.reshape(REPLICAS, ROWS), appended[:, :, 0].reshape(REPLICAS, ROWS, STEPS, KVH, HEAD), appended[:, :, 1].reshape(REPLICAS, ROWS, STEPS, KVH, HEAD))
    attended = lax.map(one_replica, bundle).reshape(ROWS_ALL, STEPS, QH * HEAD)
    return (attended, appended.reshape(ROWS_ALL, STEPS, 2, KVH * HEAD))
```

```python
import functools

import jax
import jax.numpy as jnp
from jax import lax
from jax.experimental import pallas as pl
from jax.experimental.pallas import tpu as pltpu
from jax.sharding import PartitionSpec as P

HEAD = 128
GROUP = 4
NEG = -1e30

epsilon = 1e-06


def cached_kernel(lengths, q_ref, k_ref, v_ref, *rest):
    qr_ref, acc_ref, stat_ref = rest[-3:]
    length = lengths[pl.program_id(0)]
    steps = q_ref.shape[1]
    context = k_ref.shape[1]
    heads = k_ref.shape[2] // HEAD
    per = q_ref.shape[2] // (heads * HEAD)
    scaling = HEAD ** (-0.5)
    visible = lax.broadcasted_iota(jnp.int32, (per * steps, context), 1) < length
    lane = lax.broadcasted_iota(jnp.int32, (per * steps, HEAD), 1)
    for h in range(heads):
        q = jnp.concatenate(
            [
                q_ref[0, :, (h * per + g) * HEAD : (h * per + g + 1) * HEAD].astype(jnp.float32)
                for g in range(per)
            ],
            axis=0,
        ).astype(jnp.bfloat16)
        qr_ref[0, h] = q
        cols = slice(h * HEAD, (h + 1) * HEAD)
        scores = (
            lax.dot_general(
                q, k_ref[0, :, cols], (((1,), (1,)), ((), ())), preferred_element_type=jnp.float32
            )
            * scaling
        )
        scores = jnp.where(visible, scores, NEG)
        highest = jnp.max(scores, axis=-1, keepdims=True)
        weights = jnp.where(visible, jnp.exp(scores - highest), 0.0)
        total = jnp.sum(weights, axis=-1, keepdims=True)
        acc_ref[0, h] = jnp.dot(
            weights.astype(jnp.bfloat16), v_ref[0, :, cols], preferred_element_type=jnp.float32
        )
        stat_ref[0, h] = jnp.where(lane < HEAD // 2, highest, total)


def cached_attention(queries, key_cache, value_cache, lengths, after):
    rows, steps, width = queries.shape
    context, local = key_cache.shape[1:]
    heads = local // HEAD
    count = width // (heads * HEAD) * steps
    block = lambda *shape: pl.BlockSpec((1,) + shape, lambda r, n: (r,) + (0,) * len(shape))
    piece = (rows, heads, count, HEAD)
    return pl.pallas_call(
        cached_kernel,
        grid_spec=pltpu.PrefetchScalarGridSpec(
            num_scalar_prefetch=1,
            grid=(rows,),
            in_specs=[block(steps, width), block(context, local), block(context, local)]
            + [pl.BlockSpec(memory_space=pl.ANY)] * len(after),
            out_specs=[block(heads, count, HEAD)] * 3,
        ),
        out_shape=(
            jax.ShapeDtypeStruct(piece, jnp.bfloat16),
            jax.ShapeDtypeStruct(piece, jnp.float32),
            jax.ShapeDtypeStruct(piece, jnp.float32),
        ),
        cost_estimate=pl.CostEstimate(
            flops=4 * rows * heads * count * context * HEAD,
            bytes_accessed=4 * rows * context * local + 14 * rows * heads * count * HEAD,
            transcendentals=rows * heads * count * context,
        ),
    )(lengths, queries, key_cache, value_cache, *after)


def final_kernel(adopt, qr_ref, acc_ref, stat_ref, sk, sv, ok, ov, rk, rv, out_ref, nk_ref, nv_ref):
    rows, _, count, _ = qr_ref.shape
    flat = sk.shape[0]
    steps = flat // rows
    step = lax.rem(lax.broadcasted_iota(jnp.int32, (flat, HEAD), 0), steps)
    fresh = step >= adopt[0]
    current_k = ok[...]
    current_v = ov[...]
    for d in range(rk.shape[0]):
        current_k = current_k + rk[d].astype(jnp.float32)
        current_v = current_v + rv[d].astype(jnp.float32)
    keys = jnp.where(fresh, current_k, sk[...])
    values = jnp.where(fresh, current_v, sv[...])
    keys = keys * lax.rsqrt(jnp.mean(keys * keys, axis=-1, keepdims=True) + epsilon)
    keys = keys.astype(jnp.bfloat16)
    values = values.astype(jnp.bfloat16)
    nk_ref[...] = keys
    nv_ref[...] = values
    every = rows * count
    q = qr_ref[...].reshape(every, HEAD)
    acc = acc_ref[...].reshape(every, HEAD)
    stat = stat_ref[...].reshape(every, HEAD)
    highest = stat[:, :1]
    total = stat[:, HEAD // 2 : HEAD // 2 + 1]
    scores = lax.dot_general(
        q, keys, (((1,), (1,)), ((), ())), preferred_element_type=jnp.float32
    ) * (HEAD ** (-0.5))
    i = lax.broadcasted_iota(jnp.int32, (every, flat), 0)
    j = lax.broadcasted_iota(jnp.int32, (every, flat), 1)
    visible = (i // count == j // steps) & (lax.rem(j, steps) <= lax.rem(i, steps))
    scores = jnp.where(visible, scores, NEG)
    top = jnp.maximum(highest, jnp.max(scores, axis=-1, keepdims=True))
    weights = jnp.where(visible, jnp.exp(scores - top), 0.0)
    decay = jnp.exp(highest - top)
    denominator = total * decay + jnp.sum(weights, axis=-1, keepdims=True)
    mixed = acc * decay + jnp.dot(
        weights.astype(jnp.bfloat16), values, preferred_element_type=jnp.float32
    )
    mixed = (mixed / denominator).reshape(rows, count, HEAD)
    for g in range(count // steps):
        out_ref[:, :, g * HEAD : (g + 1) * HEAD] = mixed[:, g * steps : (g + 1) * steps, :].astype(
            jnp.bfloat16
        )


def final_attention(adopt, qr, acc, stat, stale, own, received):
    rows, heads, count, _ = qr.shape
    flat, both = stale.shape
    steps = flat // rows
    piece = pl.BlockSpec((rows, 1, count, HEAD), lambda h, n: (0, h, 0, 0))
    key = pl.BlockSpec((flat, HEAD), lambda h, n: (0, h))
    value = pl.BlockSpec((flat, HEAD), lambda h, n: (0, heads + h))
    others = received.shape[0]
    rkey = pl.BlockSpec((others, flat, HEAD), lambda h, n: (0, 0, h))
    rvalue = pl.BlockSpec((others, flat, HEAD), lambda h, n: (0, 0, heads + h))
    per = count // steps
    return pl.pallas_call(
        final_kernel,
        grid_spec=pltpu.PrefetchScalarGridSpec(
            num_scalar_prefetch=1,
            grid=(heads,),
            in_specs=[piece] * 3 + [key, value, key, value, rkey, rvalue],
            out_specs=[
                pl.BlockSpec((rows, steps, per * HEAD), lambda h, n: (0, 0, h)),
                key,
                key,
            ],
        ),
        out_shape=(
            jax.ShapeDtypeStruct((rows, steps, heads * per * HEAD), jnp.bfloat16),
            jax.ShapeDtypeStruct((flat, both // 2), jnp.bfloat16),
            jax.ShapeDtypeStruct((flat, both // 2), jnp.bfloat16),
        ),
        compiler_params=pltpu.CompilerParams(vmem_limit_bytes=40 * 1024 * 1024),
        cost_estimate=pl.CostEstimate(
            flops=4 * rows * heads * count * flat * HEAD,
            bytes_accessed=12 * rows * heads * count * HEAD,
            transcendentals=rows * heads * count * flat,
        ),
    )(adopt, qr, acc, stat, stale, stale, own, own, received, received)


def on_device(replicas, parts, hidden, queries, key_cache, value_cache, lengths, adopt, old_kv, fresh_kv):
    outer = replicas // GROUP
    rows, steps, share = hidden.shape
    width = share * parts
    flat = rows * steps
    both = 2 * old_kv.shape[2]
    plane = lax.axis_index("rep") // GROUP

    piece = fresh_kv.reshape(fresh_kv.shape[0], both)
    groups = [[z * GROUP + p for p in range(GROUP)] for z in range(outer)]
    weights = lax.all_gather(piece, "rep", axis=0, tiled=True, axis_index_groups=groups)

    mine = hidden.reshape(flat, share)
    me = lax.axis_index("tp")
    whole = jnp.zeros((flat, width), jnp.bfloat16)
    whole = lax.dynamic_update_slice(whole, mine, (0, me * share))
    for d in range(1, parts):
        got = lax.ppermute(mine, "tp", [(t, (t + d) % parts) for t in range(parts)])
        whole = lax.dynamic_update_slice(whole, got, (0, lax.rem(me - d + parts, parts) * share))
    widened = whole.astype(jnp.float32)
    normed = (
        widened * lax.rsqrt(jnp.mean(widened * widened, axis=-1, keepdims=True) + epsilon)
    ).astype(jnp.bfloat16)

    depth = width // outer

    def shift(d):
        return [
            (z * GROUP + p, (z + d) % outer * GROUP + p) for z in range(outer) for p in range(GROUP)
        ]

    def columns(z):
        return lax.dynamic_slice(normed, (0, z * depth), (flat, depth))

    inputs = [columns(plane)]
    for d in range(1, outer):
        inputs.append(lax.ppermute(columns(lax.rem(plane + d, outer)), "rep", shift(d)))
    own = jnp.dot(inputs[0], weights, preferred_element_type=jnp.float32)
    received = []
    sent = []
    for d in range(1, outer):
        partial = jnp.dot(inputs[d], weights, preferred_element_type=jnp.float32)
        sent.append(partial.astype(jnp.bfloat16))
        received.append(lax.ppermute(sent[-1], "rep", shift(outer - d)))
    received = jnp.stack(received)

    old_kv, _ = lax.optimization_barrier((old_kv, normed[:1, :1]))
    stale = jnp.dot(normed, old_kv.reshape(width, both), preferred_element_type=jnp.float32)
    qr, acc, stat = cached_attention(queries, key_cache, value_cache, lengths, sent)
    attended, keys, values = final_attention(adopt, qr, acc, stat, stale, own, received)
    appended = jnp.stack([keys, values], axis=1).reshape(rows, steps, 2, both // 2)
    return attended, appended


def solution(mesh):
    placed = (
        P("rep", None, "tp"),
        P("rep", None, "tp"),
        P("rep", None, "tp"),
        P("rep", None, "tp"),
        P("rep"),
        P("rep"),
        P(None, None, "tp"),
        P("rep", None, "tp"),
    )
    return jax.shard_map(
        functools.partial(on_device, mesh.shape["rep"], mesh.shape["tp"]),
        mesh=mesh,
        in_specs=placed,
        out_specs=(P("rep", None, "tp"), P("rep", None, None, "tp")),
        check_vma=False,
    )
```

```python
import functools
import math

import jax
import jax.numpy as jnp
from jax import lax
from jax.experimental import pallas as pl
from jax.experimental.pallas import tpu as pltpu
from jax.sharding import PartitionSpec as P

HEAD = 128
GROUP = 4
NEG = -1e30
TO_EXP2 = HEAD ** (-0.5) * math.log2(math.e)

epsilon = 1e-06


def cached_kernel(lengths, q_ref, k_ref, v_ref, *rest):
    qr_ref, acc_ref, stat_ref = rest[-3:]
    rows, steps = q_ref.shape[:2]
    context = k_ref.shape[1]
    heads = k_ref.shape[2] // HEAD
    per = q_ref.shape[2] // (heads * HEAD)
    first = pl.program_id(0) * rows
    position = lax.broadcasted_iota(jnp.int32, (per * steps, context), 1)
    lane = lax.broadcasted_iota(jnp.int32, (per * steps, HEAD), 1)
    for r in range(rows):
        visible = position < lengths[first + r]
        wide = q_ref[r].astype(jnp.float32)
        for h in range(heads):
            q = jnp.concatenate(
                [wide[:, (h * per + g) * HEAD : (h * per + g + 1) * HEAD] for g in range(per)],
                axis=0,
            ).astype(jnp.bfloat16)
            qr_ref[r, h] = q
            cols = slice(h * HEAD, (h + 1) * HEAD)
            scores = lax.dot_general(
                q, k_ref[r, :, cols], (((1,), (1,)), ((), ())), preferred_element_type=jnp.float32
            )
            scores = jnp.where(visible, scores, NEG)
            highest = jnp.max(scores, axis=-1, keepdims=True)
            weights = jnp.exp2((scores - highest) * TO_EXP2)
            total = jnp.sum(weights, axis=-1, keepdims=True)
            acc_ref[r, h] = jnp.dot(
                weights.astype(jnp.bfloat16), v_ref[r, :, cols], preferred_element_type=jnp.float32
            )
            stat_ref[r, h] = jnp.where(lane < HEAD // 2, highest, total)


def cached_attention(queries, key_cache, value_cache, lengths, after):
    rows, steps, width = queries.shape
    context, local = key_cache.shape[1:]
    heads = local // HEAD
    count = width // (heads * HEAD) * steps
    some = 4 if rows % 4 == 0 else 1
    block = lambda *shape: pl.BlockSpec((some,) + shape, lambda r, n: (r,) + (0,) * len(shape))
    piece = (rows, heads, count, HEAD)
    return pl.pallas_call(
        cached_kernel,
        grid_spec=pltpu.PrefetchScalarGridSpec(
            num_scalar_prefetch=1,
            grid=(rows // some,),
            in_specs=[block(steps, width), block(context, local), block(context, local)]
            + [pl.BlockSpec(memory_space=pl.ANY)] * len(after),
            out_specs=[block(heads, count, HEAD)] * 3,
        ),
        out_shape=(
            jax.ShapeDtypeStruct(piece, jnp.bfloat16),
            jax.ShapeDtypeStruct(piece, jnp.float32),
            jax.ShapeDtypeStruct(piece, jnp.float32),
        ),
        compiler_params=pltpu.CompilerParams(vmem_limit_bytes=32 * 1024 * 1024),
        cost_estimate=pl.CostEstimate(
            flops=4 * rows * heads * count * context * HEAD,
            bytes_accessed=4 * rows * context * local + 14 * rows * heads * count * HEAD,
            transcendentals=rows * heads * count * context,
        ),
    )(lengths, queries, key_cache, value_cache, *after)


def final_kernel(adopt, qr_ref, acc_ref, stat_ref, sk, sv, ok, ov, *rest):
    out_ref, nk_ref, nv_ref = rest[-3:]
    received = rest[:-3]
    rows, _, count, _ = qr_ref.shape
    flat = sk.shape[0]
    steps = flat // rows
    step = lax.rem(lax.broadcasted_iota(jnp.int32, (flat, HEAD), 0), steps)
    fresh = step >= adopt[0]
    current_k = ok[...]
    current_v = ov[...]
    for d in range(len(received) // 2):
        current_k = current_k + received[2 * d][...].astype(jnp.float32)
        current_v = current_v + received[2 * d + 1][...].astype(jnp.float32)
    keys = jnp.where(fresh, current_k, sk[...])
    values = jnp.where(fresh, current_v, sv[...])
    keys = keys * lax.rsqrt(jnp.mean(keys * keys, axis=-1, keepdims=True) + epsilon)
    keys = keys.astype(jnp.bfloat16)
    values = values.astype(jnp.bfloat16)
    nk_ref[...] = keys
    nv_ref[...] = values
    every = rows * count
    q = qr_ref[...].reshape(every, HEAD)
    acc = acc_ref[...].reshape(every, HEAD)
    stat = stat_ref[...].reshape(every, HEAD)
    highest = stat[:, :1]
    total = stat[:, HEAD // 2 : HEAD // 2 + 1]
    scores = lax.dot_general(
        q, keys, (((1,), (1,)), ((), ())), preferred_element_type=jnp.float32
    )
    i = lax.broadcasted_iota(jnp.int32, (every, flat), 0)
    j = lax.broadcasted_iota(jnp.int32, (every, flat), 1)
    since = j - lax.shift_right_logical(i, count.bit_length() - 1) * steps
    visible = (since >= 0) & (since <= (i & (steps - 1)))
    scores = jnp.where(visible, scores, NEG)
    top = jnp.maximum(highest, jnp.max(scores, axis=-1, keepdims=True))
    weights = jnp.exp2((scores - top) * TO_EXP2)
    decay = jnp.exp2((highest - top) * TO_EXP2)
    denominator = total * decay + jnp.sum(weights, axis=-1, keepdims=True)
    mixed = acc * decay + jnp.dot(
        weights.astype(jnp.bfloat16), values, preferred_element_type=jnp.float32
    )
    mixed = (mixed * (1.0 / denominator)).reshape(rows, count, HEAD)
    for g in range(count // steps):
        out_ref[:, :, g * HEAD : (g + 1) * HEAD] = mixed[:, g * steps : (g + 1) * steps, :].astype(
            jnp.bfloat16
        )


def final_attention(adopt, qr, acc, stat, stale, own, received):
    rows, heads, count, _ = qr.shape
    flat, both = stale.shape
    steps = flat // rows
    piece = pl.BlockSpec((rows, 1, count, HEAD), lambda h, n: (0, h, 0, 0))
    key = pl.BlockSpec((flat, HEAD), lambda h, n: (0, h))
    value = pl.BlockSpec((flat, HEAD), lambda h, n: (0, heads + h))
    doubled = [array for array in received for _ in range(2)]
    per = count // steps
    return pl.pallas_call(
        final_kernel,
        grid_spec=pltpu.PrefetchScalarGridSpec(
            num_scalar_prefetch=1,
            grid=(heads,),
            in_specs=[piece] * 3 + [key, value] * (2 + len(received)),
            out_specs=[
                pl.BlockSpec((rows, steps, per * HEAD), lambda h, n: (0, 0, h)),
                key,
                key,
            ],
        ),
        out_shape=(
            jax.ShapeDtypeStruct((rows, steps, heads * per * HEAD), jnp.bfloat16),
            jax.ShapeDtypeStruct((flat, both // 2), jnp.bfloat16),
            jax.ShapeDtypeStruct((flat, both // 2), jnp.bfloat16),
        ),
        compiler_params=pltpu.CompilerParams(vmem_limit_bytes=40 * 1024 * 1024),
        cost_estimate=pl.CostEstimate(
            flops=4 * rows * heads * count * flat * HEAD,
            bytes_accessed=12 * rows * heads * count * HEAD,
            transcendentals=rows * heads * count * flat,
        ),
    )(adopt, qr, acc, stat, stale, stale, own, own, *doubled)


def on_device(replicas, parts, hidden, queries, key_cache, value_cache, lengths, adopt, old_kv, fresh_kv):
    outer = replicas // GROUP
    rows, steps, share = hidden.shape
    width = share * parts
    flat = rows * steps
    both = 2 * old_kv.shape[2]
    plane = lax.axis_index("rep") // GROUP

    piece = fresh_kv.reshape(fresh_kv.shape[0], both)
    count = fresh_kv.shape[0]
    spot = lax.axis_index("rep") % GROUP
    weights = jnp.zeros((GROUP * count, both), jnp.bfloat16)
    weights = lax.dynamic_update_slice(weights, piece, (spot * count, 0))
    for k in range(1, GROUP):
        got = lax.ppermute(piece, "rep", [(r, r ^ k) for r in range(replicas)])
        weights = lax.dynamic_update_slice(weights, got, ((spot ^ k) * count, 0))

    mine = hidden.reshape(flat, share)
    me = lax.axis_index("tp")
    whole = jnp.zeros((flat, width), jnp.bfloat16)
    whole = lax.dynamic_update_slice(whole, mine, (0, me * share))
    for d in range(1, parts):
        got = lax.ppermute(mine, "tp", [(t, (t + d) % parts) for t in range(parts)])
        whole = lax.dynamic_update_slice(whole, got, (0, lax.rem(me - d + parts, parts) * share))
    widened = whole.astype(jnp.float32)
    normed = (
        widened * lax.rsqrt(jnp.mean(widened * widened, axis=-1, keepdims=True) + epsilon)
    ).astype(jnp.bfloat16)

    depth = width // outer

    def shift(d):
        return [
            (z * GROUP + p, (z + d) % outer * GROUP + p) for z in range(outer) for p in range(GROUP)
        ]

    def columns(z):
        return lax.dynamic_slice(normed, (0, z * depth), (flat, depth))

    inputs = [columns(plane)]
    for d in range(1, outer):
        inputs.append(lax.ppermute(columns(lax.rem(plane + d, outer)), "rep", shift(d)))
    own = jnp.dot(inputs[0], weights, preferred_element_type=jnp.float32)
    received = []
    sent = []
    for d in range(1, outer):
        partial = jnp.dot(inputs[d], weights, preferred_element_type=jnp.float32)
        sent.append(partial.astype(jnp.bfloat16))
        received.append(lax.ppermute(sent[-1], "rep", shift(outer - d)))

    old_kv, _ = lax.optimization_barrier((old_kv, normed[:1, :1]))
    stale = jnp.dot(normed, old_kv.reshape(width, both), preferred_element_type=jnp.float32)
    qr, acc, stat = cached_attention(queries, key_cache, value_cache, lengths, sent)
    attended, keys, values = final_attention(adopt, qr, acc, stat, stale, own, received)
    appended = jnp.stack([keys, values], axis=1).reshape(rows, steps, 2, both // 2)
    return attended, appended


def solution(mesh):
    placed = (
        P("rep", None, "tp"),
        P("rep", None, "tp"),
        P("rep", None, "tp"),
        P("rep", None, "tp"),
        P("rep"),
        P("rep"),
        P(None, None, "tp"),
        P("rep", None, "tp"),
    )
    return jax.shard_map(
        functools.partial(on_device, mesh.shape["rep"], mesh.shape["tp"]),
        mesh=mesh,
        in_specs=placed,
        out_specs=(P("rep", None, "tp"), P("rep", None, None, "tp")),
        check_vma=False,
    )
```

```python
import functools
import math

import jax
import jax.numpy as jnp
from jax import lax
from jax.experimental import pallas as pl
from jax.experimental.pallas import tpu as pltpu
from jax.sharding import PartitionSpec as P

HEAD = 128
GROUP = 4
NEG = -1e30
TO_EXP2 = HEAD ** (-0.5) * math.log2(math.e)

epsilon = 1e-06


def cached_kernel(start, lengths, q_ref, k_ref, v_ref, *rest):
    qr_ref, acc_ref, stat_ref = rest[-3:]
    rows, steps = q_ref.shape[:2]
    context = k_ref.shape[1]
    heads = k_ref.shape[2] // HEAD
    per = q_ref.shape[2] // (heads * HEAD)
    first = start + pl.program_id(0) * rows
    position = lax.broadcasted_iota(jnp.int32, (per * steps, context), 1)
    lane = lax.broadcasted_iota(jnp.int32, (per * steps, HEAD), 1)
    for r in range(rows):
        visible = position < lengths[first + r]
        wide = q_ref[r].astype(jnp.float32)
        for h in range(heads):
            q = jnp.concatenate(
                [wide[:, (h * per + g) * HEAD : (h * per + g + 1) * HEAD] for g in range(per)],
                axis=0,
            ).astype(jnp.bfloat16)
            qr_ref[r, h] = q
            cols = slice(h * HEAD, (h + 1) * HEAD)
            scores = lax.dot_general(
                q, k_ref[r, :, cols], (((1,), (1,)), ((), ())), preferred_element_type=jnp.float32
            )
            scores = jnp.where(visible, scores, NEG)
            highest = jnp.max(scores, axis=-1, keepdims=True)
            weights = jnp.exp2((scores - highest) * TO_EXP2)
            total = jnp.sum(weights, axis=-1, keepdims=True)
            acc_ref[r, h] = jnp.dot(
                weights.astype(jnp.bfloat16), v_ref[r, :, cols], preferred_element_type=jnp.float32
            )
            stat_ref[r, h] = jnp.where(lane < HEAD // 2, highest, total)


def cached_attention(queries, key_cache, value_cache, lengths, start, taken, after, held):
    rows, steps, width = queries.shape
    context, local = key_cache.shape[1:]
    heads = local // HEAD
    count = width // (heads * HEAD) * steps
    some = 4 if start % 4 == 0 and taken % 4 == 0 else 1
    skip = start // some
    block = lambda *shape: pl.BlockSpec((some,) + shape, lambda r, n: (skip + r,) + (0,) * len(shape))
    piece = (rows, heads, count, HEAD)
    return pl.pallas_call(
        functools.partial(cached_kernel, start),
        grid_spec=pltpu.PrefetchScalarGridSpec(
            num_scalar_prefetch=1,
            grid=(taken // some,),
            in_specs=[block(steps, width), block(context, local), block(context, local)]
            + [pl.BlockSpec(memory_space=pl.ANY)] * (len(after) + len(held)),
            out_specs=[block(heads, count, HEAD)] * 3,
        ),
        out_shape=(
            jax.ShapeDtypeStruct(piece, jnp.bfloat16),
            jax.ShapeDtypeStruct(piece, jnp.float32),
            jax.ShapeDtypeStruct(piece, jnp.float32),
        ),
        input_output_aliases={4 + len(after) + i: i for i in range(len(held))},
        compiler_params=pltpu.CompilerParams(vmem_limit_bytes=32 * 1024 * 1024),
        cost_estimate=pl.CostEstimate(
            flops=4 * taken * heads * count * context * HEAD,
            bytes_accessed=4 * taken * context * local + 14 * taken * heads * count * HEAD,
            transcendentals=taken * heads * count * context,
        ),
    )(lengths, queries, key_cache, value_cache, *after, *held)


def final_kernel(adopt, qr_ref, acc_ref, stat_ref, norm_ref, sk, sv, ok, ov, *rest):
    out_ref, nk_ref, nv_ref = rest[-3:]
    received = rest[:-3]
    rows, _, count, _ = qr_ref.shape
    flat = sk.shape[0]
    steps = flat // rows
    step = lax.rem(lax.broadcasted_iota(jnp.int32, (flat, HEAD), 0), steps)
    fresh = step >= adopt[0]
    current_k = ok[...]
    current_v = ov[...]
    for d in range(len(received) // 2):
        current_k = current_k + received[2 * d][...].astype(jnp.float32)
        current_v = current_v + received[2 * d + 1][...].astype(jnp.float32)
    keys = jnp.where(fresh, current_k * norm_ref[...], sk[...])
    values = jnp.where(fresh, current_v * norm_ref[...], sv[...])
    keys = keys * lax.rsqrt(jnp.mean(keys * keys, axis=-1, keepdims=True) + epsilon)
    keys = keys.astype(jnp.bfloat16)
    values = values.astype(jnp.bfloat16)
    nk_ref[...] = keys
    nv_ref[...] = values
    every = rows * count
    q = qr_ref[...].reshape(every, HEAD)
    acc = acc_ref[...].reshape(every, HEAD)
    stat = stat_ref[...].reshape(every, HEAD)
    highest = stat[:, :1]
    total = stat[:, HEAD // 2 : HEAD // 2 + 1]
    scores = lax.dot_general(
        q, keys, (((1,), (1,)), ((), ())), preferred_element_type=jnp.float32
    )
    i = lax.broadcasted_iota(jnp.int32, (every, flat), 0)
    j = lax.broadcasted_iota(jnp.int32, (every, flat), 1)
    since = j - lax.shift_right_logical(i, count.bit_length() - 1) * steps
    visible = (since >= 0) & (since <= (i & (steps - 1)))
    scores = jnp.where(visible, scores, NEG)
    top = jnp.maximum(highest, jnp.max(scores, axis=-1, keepdims=True))
    weights = jnp.exp2((scores - top) * TO_EXP2)
    decay = jnp.exp2((highest - top) * TO_EXP2)
    denominator = total * decay + jnp.sum(weights, axis=-1, keepdims=True)
    mixed = acc * decay + jnp.dot(
        weights.astype(jnp.bfloat16), values, preferred_element_type=jnp.float32
    )
    mixed = (mixed * (1.0 / denominator)).reshape(rows, count, HEAD)
    for g in range(count // steps):
        out_ref[:, :, g * HEAD : (g + 1) * HEAD] = mixed[:, g * steps : (g + 1) * steps, :].astype(
            jnp.bfloat16
        )


def final_attention(adopt, qr, acc, stat, norm, stale, own, received):
    rows, heads, count, _ = qr.shape
    flat, both = stale.shape
    steps = flat // rows
    piece = pl.BlockSpec((rows, 1, count, HEAD), lambda h, n: (0, h, 0, 0))
    key = pl.BlockSpec((flat, HEAD), lambda h, n: (0, h))
    value = pl.BlockSpec((flat, HEAD), lambda h, n: (0, heads + h))
    doubled = [array for array in received for _ in range(2)]
    per = count // steps
    return pl.pallas_call(
        final_kernel,
        grid_spec=pltpu.PrefetchScalarGridSpec(
            num_scalar_prefetch=1,
            grid=(heads,),
            in_specs=[piece] * 3 + [pl.BlockSpec((flat, HEAD), lambda h, n: (0, 0))] + [key, value] * (2 + len(received)),
            out_specs=[
                pl.BlockSpec((rows, steps, per * HEAD), lambda h, n: (0, 0, h)),
                key,
                key,
            ],
        ),
        out_shape=(
            jax.ShapeDtypeStruct((rows, steps, heads * per * HEAD), jnp.bfloat16),
            jax.ShapeDtypeStruct((flat, both // 2), jnp.bfloat16),
            jax.ShapeDtypeStruct((flat, both // 2), jnp.bfloat16),
        ),
        compiler_params=pltpu.CompilerParams(vmem_limit_bytes=40 * 1024 * 1024),
        cost_estimate=pl.CostEstimate(
            flops=4 * rows * heads * count * flat * HEAD,
            bytes_accessed=12 * rows * heads * count * HEAD,
            transcendentals=rows * heads * count * flat,
        ),
    )(adopt, qr, acc, stat, norm, stale, stale, own, own, *doubled)


def on_device(replicas, parts, hidden, queries, key_cache, value_cache, lengths, adopt, old_kv, fresh_kv):
    outer = replicas // GROUP
    rows, steps, share = hidden.shape
    width = share * parts
    flat = rows * steps
    both = 2 * old_kv.shape[2]
    plane = lax.axis_index("rep") // GROUP

    piece = fresh_kv.reshape(fresh_kv.shape[0], both)
    count = fresh_kv.shape[0]
    spot = lax.axis_index("rep") % GROUP
    weights = jnp.zeros((GROUP * count, both), jnp.bfloat16)
    weights = lax.dynamic_update_slice(weights, piece, (spot * count, 0))
    for k in range(1, GROUP):
        got = lax.ppermute(piece, "rep", [(r, r ^ k) for r in range(replicas)])
        weights = lax.dynamic_update_slice(weights, got, ((spot ^ k) * count, 0))

    mine = hidden.reshape(flat, share)
    me = lax.axis_index("tp")
    depth = width // outer
    planes = outer // parts

    def shift(d):
        return [
            (z * GROUP + p, (z + d) % outer * GROUP + p) for z in range(outer) for p in range(GROUP)
        ]

    def holders(d):
        pairs = []
        for source, target in shift(d):
            t = target // GROUP // planes
            pairs.append((source * parts + t, target * parts + t))
        return pairs

    inputs = []
    for d in range(outer):
        z = lax.rem(plane + d, outer)
        block = lax.dynamic_slice(mine, (0, lax.rem(z, planes) * depth), (flat, depth))
        if d == 0:
            block = jnp.where(me == plane // planes, block, jnp.zeros_like(block))
        else:
            block = lax.ppermute(block, ("rep", "tp"), holders(d))
        inputs.append(block)
    if parts == 2:
        inputs = [block + lax.ppermute(block, "tp", [(0, 1), (1, 0)]) for block in inputs]
    else:
        inputs = [lax.psum(block, "tp") for block in inputs]

    whole = jnp.zeros((flat, width), jnp.bfloat16)
    whole = lax.dynamic_update_slice(whole, mine, (0, me * share))
    for d in range(1, parts):
        got = lax.ppermute(mine, "tp", [(t, (t + d) % parts) for t in range(parts)])
        whole = lax.dynamic_update_slice(whole, got, (0, lax.rem(me - d + parts, parts) * share))
    widened = whole.astype(jnp.float32)
    norm = lax.rsqrt(jnp.mean(widened * widened, axis=-1, keepdims=True) + epsilon)
    normed = (widened * norm).astype(jnp.bfloat16)

    own = jnp.dot(inputs[0], weights, preferred_element_type=jnp.float32)
    received = []
    sent = []
    for d in range(1, outer):
        partial = jnp.dot(inputs[d], weights, preferred_element_type=jnp.float32)
        sent.append(partial.astype(jnp.bfloat16))
        received.append(lax.ppermute(sent[-1], "rep", shift(outer - d)))

    stale = jnp.dot(normed, old_kv.reshape(width, both), preferred_element_type=jnp.float32)
    early = 3 * rows // 8
    held = cached_attention(queries, key_cache, value_cache, lengths, 0, early, [], ())
    qr, acc, stat = cached_attention(
        queries, key_cache, value_cache, lengths, early, rows - early, sent, held
    )
    norm = jnp.broadcast_to(norm, (flat, HEAD))
    attended, keys, values = final_attention(adopt, qr, acc, stat, norm, stale, own, received)
    appended = jnp.stack([keys, values], axis=1).reshape(rows, steps, 2, both // 2)
    return attended, appended


def solution(mesh):
    placed = (
        P("rep", None, "tp"),
        P("rep", None, "tp"),
        P("rep", None, "tp"),
        P("rep", None, "tp"),
        P("rep"),
        P("rep"),
        P(None, None, "tp"),
        P("rep", None, "tp"),
    )
    return jax.shard_map(
        functools.partial(on_device, mesh.shape["rep"], mesh.shape["tp"]),
        mesh=mesh,
        in_specs=placed,
        out_specs=(P("rep", None, "tp"), P("rep", None, None, "tp")),
        check_vma=False,
    )
```

```python
import functools
import math

import jax
import jax.numpy as jnp
from jax import lax
from jax.experimental import pallas as pl
from jax.experimental.pallas import tpu as pltpu
from jax.sharding import PartitionSpec as P

HEAD = 128
GROUP = 4
NEG = -1e30
TO_EXP2 = HEAD ** (-0.5) * math.log2(math.e)

epsilon = 1e-06


def cached_kernel(start, lengths, q_ref, k_ref, v_ref, *rest):
    qr_ref, acc_ref, stat_ref = rest[-3:]
    rows, steps = q_ref.shape[:2]
    context = k_ref.shape[1]
    heads = k_ref.shape[2] // HEAD
    per = q_ref.shape[2] // (heads * HEAD)
    first = start + pl.program_id(0) * rows
    position = lax.broadcasted_iota(jnp.int32, (per * steps, context), 1)
    lane = lax.broadcasted_iota(jnp.int32, (per * steps, HEAD), 1)
    for r in range(rows):
        visible = position < lengths[first + r]
        wide = q_ref[r].astype(jnp.float32)
        for h in range(heads):
            q = jnp.concatenate(
                [wide[:, (h * per + g) * HEAD : (h * per + g + 1) * HEAD] for g in range(per)],
                axis=0,
            ).astype(jnp.bfloat16)
            qr_ref[r, h] = q
            cols = slice(h * HEAD, (h + 1) * HEAD)
            scores = lax.dot_general(
                q, k_ref[r, :, cols], (((1,), (1,)), ((), ())), preferred_element_type=jnp.float32
            )
            scores = jnp.where(visible, scores, NEG)
            highest = jnp.max(scores, axis=-1, keepdims=True)
            weights = jnp.exp2((scores - highest) * TO_EXP2)
            total = jnp.sum(weights, axis=-1, keepdims=True)
            acc_ref[r, h] = jnp.dot(
                weights.astype(jnp.bfloat16), v_ref[r, :, cols], preferred_element_type=jnp.float32
            )
            stat_ref[r, h] = jnp.where(lane < HEAD // 2, highest, total)


def cached_attention(queries, key_cache, value_cache, lengths, start, taken, after, held):
    rows, steps, width = queries.shape
    context, local = key_cache.shape[1:]
    heads = local // HEAD
    count = width // (heads * HEAD) * steps
    some = 4 if start % 4 == 0 and taken % 4 == 0 else 1
    skip = start // some
    block = lambda *shape: pl.BlockSpec((some,) + shape, lambda r, n: (skip + r,) + (0,) * len(shape))
    piece = (rows, heads, count, HEAD)
    return pl.pallas_call(
        functools.partial(cached_kernel, start),
        grid_spec=pltpu.PrefetchScalarGridSpec(
            num_scalar_prefetch=1,
            grid=(taken // some,),
            in_specs=[block(steps, width), block(context, local), block(context, local)]
            + [pl.BlockSpec(memory_space=pl.ANY)] * (len(after) + len(held)),
            out_specs=[block(heads, count, HEAD)] * 3,
        ),
        out_shape=(
            jax.ShapeDtypeStruct(piece, jnp.bfloat16),
            jax.ShapeDtypeStruct(piece, jnp.float32),
            jax.ShapeDtypeStruct(piece, jnp.float32),
        ),
        input_output_aliases={4 + len(after) + i: i for i in range(len(held))},
        compiler_params=pltpu.CompilerParams(vmem_limit_bytes=32 * 1024 * 1024),
        cost_estimate=pl.CostEstimate(
            flops=4 * taken * heads * count * context * HEAD,
            bytes_accessed=4 * taken * context * local + 14 * taken * heads * count * HEAD,
            transcendentals=taken * heads * count * context,
        ),
    )(lengths, queries, key_cache, value_cache, *after, *held)


def final_kernel(adopt, qr_ref, acc_ref, stat_ref, norm_ref, sk, sv, ok, ov, *rest):
    out_ref, nk_ref, nv_ref = rest[-3:]
    received = rest[:-3]
    rows, _, count, _ = qr_ref.shape
    flat = sk.shape[0]
    steps = flat // rows
    step = lax.rem(lax.broadcasted_iota(jnp.int32, (flat, HEAD), 0), steps)
    fresh = step >= adopt[0]
    current_k = ok[...]
    current_v = ov[...]
    for d in range(len(received) // 2):
        current_k = current_k + received[2 * d][...].astype(jnp.float32)
        current_v = current_v + received[2 * d + 1][...].astype(jnp.float32)
    keys = jnp.where(fresh, current_k * norm_ref[...], sk[...])
    values = jnp.where(fresh, current_v * norm_ref[...], sv[...])
    keys = keys * lax.rsqrt(jnp.mean(keys * keys, axis=-1, keepdims=True) + epsilon)
    keys = keys.astype(jnp.bfloat16)
    values = values.astype(jnp.bfloat16)
    nk_ref[...] = keys
    nv_ref[...] = values
    every = rows * count
    q = qr_ref[...].reshape(every, HEAD)
    acc = acc_ref[...].reshape(every, HEAD)
    stat = stat_ref[...].reshape(every, HEAD)
    highest = stat[:, :1]
    total = stat[:, HEAD // 2 : HEAD // 2 + 1]
    scores = lax.dot_general(
        q, keys, (((1,), (1,)), ((), ())), preferred_element_type=jnp.float32
    )
    i = lax.broadcasted_iota(jnp.int32, (every, flat), 0)
    j = lax.broadcasted_iota(jnp.int32, (every, flat), 1)
    since = j - lax.shift_right_logical(i, count.bit_length() - 1) * steps
    visible = (since >= 0) & (since <= (i & (steps - 1)))
    scores = jnp.where(visible, scores, NEG)
    top = jnp.maximum(highest, jnp.max(scores, axis=-1, keepdims=True))
    weights = jnp.exp2((scores - top) * TO_EXP2)
    decay = jnp.exp2((highest - top) * TO_EXP2)
    denominator = total * decay + jnp.sum(weights, axis=-1, keepdims=True)
    mixed = acc * decay + jnp.dot(
        weights.astype(jnp.bfloat16), values, preferred_element_type=jnp.float32
    )
    mixed = (mixed * (1.0 / denominator)).reshape(rows, count, HEAD)
    for g in range(count // steps):
        out_ref[:, :, g * HEAD : (g + 1) * HEAD] = mixed[:, g * steps : (g + 1) * steps, :].astype(
            jnp.bfloat16
        )


def final_attention(adopt, qr, acc, stat, norm, stale, own, received):
    rows, heads, count, _ = qr.shape
    flat, both = stale.shape
    steps = flat // rows
    piece = pl.BlockSpec((rows, 1, count, HEAD), lambda h, n: (0, h, 0, 0))
    key = pl.BlockSpec((flat, HEAD), lambda h, n: (0, h))
    value = pl.BlockSpec((flat, HEAD), lambda h, n: (0, heads + h))
    doubled = [array for array in received for _ in range(2)]
    per = count // steps
    return pl.pallas_call(
        final_kernel,
        grid_spec=pltpu.PrefetchScalarGridSpec(
            num_scalar_prefetch=1,
            grid=(heads,),
            in_specs=[piece] * 3 + [pl.BlockSpec((flat, HEAD), lambda h, n: (0, 0))] + [key, value] * (2 + len(received)),
            out_specs=[
                pl.BlockSpec((rows, steps, per * HEAD), lambda h, n: (0, 0, h)),
                key,
                key,
            ],
        ),
        out_shape=(
            jax.ShapeDtypeStruct((rows, steps, heads * per * HEAD), jnp.bfloat16),
            jax.ShapeDtypeStruct((flat, both // 2), jnp.bfloat16),
            jax.ShapeDtypeStruct((flat, both // 2), jnp.bfloat16),
        ),
        compiler_params=pltpu.CompilerParams(vmem_limit_bytes=40 * 1024 * 1024),
        cost_estimate=pl.CostEstimate(
            flops=4 * rows * heads * count * flat * HEAD,
            bytes_accessed=12 * rows * heads * count * HEAD,
            transcendentals=rows * heads * count * flat,
        ),
    )(adopt, qr, acc, stat, norm, stale, stale, own, own, *doubled)


def on_device(replicas, parts, hidden, queries, key_cache, value_cache, lengths, adopt, old_kv, fresh_kv):
    outer = replicas // GROUP
    rows, steps, share = hidden.shape
    width = share * parts
    flat = rows * steps
    both = 2 * old_kv.shape[2]
    plane = lax.axis_index("rep") // GROUP

    piece = fresh_kv.reshape(fresh_kv.shape[0], both)
    count = fresh_kv.shape[0]
    spot = lax.axis_index("rep") % GROUP
    weights = jnp.zeros((GROUP * count, both), jnp.bfloat16)
    weights = lax.dynamic_update_slice(weights, piece, (spot * count, 0))
    for k in range(1, GROUP):
        got = lax.ppermute(piece, "rep", [(r, r ^ k) for r in range(replicas)])
        weights = lax.dynamic_update_slice(weights, got, ((spot ^ k) * count, 0))

    mine = hidden.reshape(flat, share)
    me = lax.axis_index("tp")
    depth = width // outer
    planes = outer // parts

    def shift(d):
        return [
            (z * GROUP + p, (z + d) % outer * GROUP + p) for z in range(outer) for p in range(GROUP)
        ]

    def holders(d):
        pairs = []
        for source, target in shift(d):
            t = target // GROUP // planes
            pairs.append((source * parts + t, target * parts + t))
        return pairs

    inputs = []
    for d in range(outer):
        z = lax.rem(plane + d, outer)
        block = lax.dynamic_slice(mine, (0, lax.rem(z, planes) * depth), (flat, depth))
        if d == 0:
            block = jnp.where(me == plane // planes, block, jnp.zeros_like(block))
        else:
            block = lax.ppermute(block, ("rep", "tp"), holders(d))
        inputs.append(block)
    if parts == 2:
        inputs = [block + lax.ppermute(block, "tp", [(0, 1), (1, 0)]) for block in inputs]
    else:
        inputs = [lax.psum(block, "tp") for block in inputs]

    whole = jnp.zeros((flat, width), jnp.bfloat16)
    whole = lax.dynamic_update_slice(whole, mine, (0, me * share))
    for d in range(1, parts):
        got = lax.ppermute(mine, "tp", [(t, (t + d) % parts) for t in range(parts)])
        whole = lax.dynamic_update_slice(whole, got, (0, lax.rem(me - d + parts, parts) * share))
    widened = whole.astype(jnp.float32)
    norm = lax.rsqrt(jnp.mean(widened * widened, axis=-1, keepdims=True) + epsilon)
    normed = (widened * norm).astype(jnp.bfloat16)

    own = jnp.dot(inputs[0], weights, preferred_element_type=jnp.float32)
    received = []
    sent = []
    for d in range(1, outer):
        partial = jnp.dot(inputs[d], weights, preferred_element_type=jnp.float32)
        sent.append(partial.astype(jnp.bfloat16))
        received.append(lax.ppermute(sent[-1], "rep", shift(outer - d)))

    stale = jnp.dot(normed, old_kv.reshape(width, both), preferred_element_type=jnp.float32)
    qr, acc, stat = cached_attention(
        queries, key_cache, value_cache, lengths, 0, rows, sent, ()
    )
    norm = jnp.broadcast_to(norm, (flat, HEAD))
    attended, keys, values = final_attention(adopt, qr, acc, stat, norm, stale, own, received)
    appended = jnp.stack([keys, values], axis=1).reshape(rows, steps, 2, both // 2)
    return attended, appended


def solution(mesh):
    placed = (
        P("rep", None, "tp"),
        P("rep", None, "tp"),
        P("rep", None, "tp"),
        P("rep", None, "tp"),
        P("rep"),
        P("rep"),
        P(None, None, "tp"),
        P("rep", None, "tp"),
    )
    return jax.shard_map(
        functools.partial(on_device, mesh.shape["rep"], mesh.shape["tp"]),
        mesh=mesh,
        in_specs=placed,
        out_specs=(P("rep", None, "tp"), P("rep", None, None, "tp")),
        check_vma=False,
    )
```
